32 devices in a mesh: dp: 8 (over y, x, core), expert: 4 (over z).
Axes of the slice: x: 2, y: 2, z: 4, core: 2. Of those that a mesh axis runs over, the one named last changes fastest.
Arguments:
- tokens: bfloat16 [4096, 3072], P(('dp', 'expert')), parts along dimension 0, may hold values from -6 to 6
- w_gate: bfloat16 [3072, 8192], P(None, 'expert'), may hold values from -0.109375 to 0.109375
- w_up: bfloat16 [3072, 8192], P(None, 'expert'), may hold values from -0.109375 to 0.109375
- w_down: bfloat16 [8192, 3072], P('expert'), may hold values from -0.0625 to 0.0625
- route_ids: int32 [4096, 2], P(('dp', 'expert')), parts along dimension 0, may hold values from 0 to 7, as said below
- route_prob: float32 [4096], P(('dp', 'expert')), parts along dimension 0, may hold values from 0.5 to 0.95
- slot_index: int32 [4096], P(('dp', 'expert')), parts along dimension 0, may hold values from 0 to 64, as said below
Outputs:
- mixed: bfloat16 [4096, 3072], P(('dp', 'expert')), parts along dimension 0
The draws below stay inside these ranges and needn't reach their ends.
There are 8 independent parts, one for each index of `dp`. The reference program is written for one: setup_inputs(seed, part) draws one part's arguments, and reference() takes and returns one part's arrays. A program takes and returns all parts, laid end to end along the dimension named above; an argument that names none is the same for every part. Nothing has to cross between parts.
Inputs may be any that keep to these rules, and one draw needn't show every extreme that they name: `route_ids`: each row names two different experts. `slot_index`: a token of whose two experts one is expert 0 holds its rank, in row order, among the tokens of its device that name expert 0; every other token holds 64. At most 64 of one device's 128 tokens name expert 0, and some device has exactly 64; the router's capacity of 64 tokens for expert 0 is counted over each aligned pair of 256 tokens (blocks 2k and 2k + 1) and is always filled, so those two devices have exactly 64 such tokens together.
All inputs are finite; a program needn't handle non-finite values.
Results may differ from the reference program's by a relative error of at most 0.023.
Values may be sent and summed in bfloat16 or wider, within the bound.
A program may use at most 128 MiB of HBM per device.

```python
import jax
import jax.numpy as jnp
from jax import lax

D = 3072
FF = 8192
NUM_EXPERTS = 8
TOK_DEV = 128
CAP = 64
TOKENS = 512
N_EXPERT = 4


def routing_draw(key):
    base = jax.random.fold_in(key, 77)
    blocks = TOKENS // TOK_DEV
    pairs = blocks // 2
    capacity = TOK_DEV // 2
    streams = jax.random.split(base, 6)
    level = jax.random.randint(streams[0], (pairs,), 0, 4)
    fullest = jax.random.randint(streams[1], (), 0, pairs)
    level = jnp.where(jnp.arange(pairs) == fullest, 0, level)
    table = jnp.array([capacity, capacity // 2, capacity // 4, capacity // 8], jnp.int32)
    even_counts = table[level]
    counts = jnp.stack([even_counts, capacity - even_counts], axis=1).reshape(blocks)
    order = jax.vmap(lambda one_key: jax.random.permutation(one_key, TOK_DEV))(jax.random.split(streams[2], blocks))
    routed = order < counts[:, None]
    ranking = jnp.cumsum(routed.astype(jnp.int32), axis=1) - 1
    slots = jnp.where(routed, ranking, capacity).reshape(TOKENS).astype(jnp.int32)
    other = jax.random.randint(streams[3], (TOKENS,), 1, NUM_EXPERTS)
    offset = jax.random.randint(streams[4], (TOKENS,), 1, NUM_EXPERTS - 1)
    second = 1 + (other - 1 + offset) % (NUM_EXPERTS - 1)
    flipped = jax.random.randint(streams[5], (TOKENS,), 0, 2)
    flat_routed = routed.reshape(TOKENS)
    first_column = jnp.where(flat_routed, jnp.where(flipped == 1, 0, other), other)
    second_column = jnp.where(flat_routed, jnp.where(flipped == 1, other, 0), second)
    chosen = jnp.stack([first_column, second_column], axis=1).astype(jnp.int32)
    return (chosen, slots)


def draw_route_ids(key, part):
    chosen, slots = routing_draw(key)
    return chosen


def draw_slot_index(key, part):
    chosen, slots = routing_draw(key)
    return slots


def steps_of(rng, dims, shards, smallest, high):
    loudness = 1.0
    for axis_at, blocks in shards:
        steps = jax.random.uniform(jax.random.fold_in(jax.random.fold_in(rng, 6), axis_at), (blocks,), jnp.float32, smallest / len(shards), high / len(shards))
        loudness = loudness * jnp.repeat(jnp.exp(steps), dims[axis_at] // blocks).reshape((-1,) + (1,) * (len(dims) - 1 - axis_at))
    return loudness


def bell_draw(own_key, shape, width, reach, shards=(), kind=jnp.bfloat16):
    result = jax.random.normal(own_key, shape, jnp.float32) * width
    if len(shards) > 0:
        result = steps_of(own_key, shape, shards, -0.22, 0.18) * result
    return jnp.clip(result, min=-reach, max=reach).astype(kind)


def setup_inputs(seed: int = 0, part: int = 0) -> dict:
    streams_of = jax.random.split(jax.random.key(seed), 8)
    own_keys = jax.random.split(jax.random.fold_in(streams_of[7], part), 8)
    return {
        "tokens": bell_draw(own_keys[0], (TOKENS, D), 1.0, 6.0, ((0, 4),)),
        "w_gate": bell_draw(streams_of[1], (D, FF), D ** -0.5, 0.109375, ((1, 4),)),
        "w_up": bell_draw(streams_of[2], (D, FF), D ** -0.5, 0.109375, ((1, 4),)),
        "w_down": bell_draw(streams_of[3], (FF, D), FF ** -0.5, 0.0625, ((0, 4),)),
        "route_ids": draw_route_ids(jax.random.fold_in(jax.random.fold_in(streams_of[7], part), 71), part),
        "route_prob": jnp.clip(0.5 + 0.45 * jax.random.uniform(own_keys[5], (TOKENS,), jnp.float32) ** steps_of(own_keys[5], (TOKENS,), ((0, 4),), -0.2, 0.2), 0.5, 0.95),
        "slot_index": draw_slot_index(jax.random.fold_in(jax.random.fold_in(streams_of[7], part), 71), part),
    }


def reference(tokens, w_gate, w_up, w_down, route_ids, route_prob, slot_index):
    share = jnp.where(route_ids[:, 0] == 0, route_prob, jnp.where(route_ids[:, 1] == 0, 1.0 - route_prob, 0.0))
    share = jnp.where(slot_index < CAP, share, 0.0).astype(jnp.float32)
    gate = jnp.dot(tokens, w_gate, preferred_element_type=jnp.float32)
    up = jnp.dot(tokens, w_up, preferred_element_type=jnp.float32)
    hidden = (jax.nn.silu(gate) * up).astype(jnp.bfloat16)
    group_width = FF // N_EXPERT
    hidden_groups = jnp.transpose(hidden.reshape(TOKENS, N_EXPERT, group_width), (1, 0, 2))
    down_groups = w_down.reshape(N_EXPERT, group_width, D)

    def accumulate(total, pieces):
        partial_value = jnp.dot(pieces[0], pieces[1], preferred_element_type=jnp.float32).astype(jnp.bfloat16)
        partial_value = lax.optimization_barrier(partial_value)
        return total + partial_value.astype(jnp.float32), None

    start_total = jnp.zeros((TOKENS, D), jnp.float32)
    down, _ = lax.scan(accumulate, start_total, (hidden_groups, down_groups))
    return (share[:, None] * down).astype(jnp.bfloat16)
```

```python
import functools

import jax
import jax.numpy as jnp
from jax import lax
from jax.experimental import pallas as pl
from jax.experimental.pallas import tpu as pltpu
from jax.sharding import PartitionSpec as P

MESH = pl.DeviceIdType.MESH
F32 = jnp.float32
BF16 = jnp.bfloat16


def loop(lo, hi):
    def run(body):
        def step(i, carry):
            body(i)
            return carry

        lax.fori_loop(lo, hi, step, 0)

    return run


def kernel(
    n, slot_ref, ids_ref, prob_ref, tok_ref, wg_hbm, wu_hbm, wd_hbm, out_ref,
    wg, wu, wd, own, raw, x, gacc, uacc, hid, part, rin, lin, rout, lout,
    wsem, raw_s, raw_r, x_s, x_r, r_s, r_r, l_s, l_r,
):
    me = lax.axis_index("expert")
    chunks, cap, width = own.shape
    pairs = n // 2
    hidden = hid.shape[1]
    tile = min(512, hidden)
    pair = me // 2
    odd = me % 2
    partner = me + 1 - 2 * odd
    has_left, has_right = me > 0, me < n - 1

    def weight(which, k):
        rows = pl.ds(pl.multiple_of(k * width, width), width)
        if which == 0:
            return pltpu.make_async_copy(wg_hbm.at[rows, :], wg.at[k], wsem.at[0, k])
        if which == 1:
            return pltpu.make_async_copy(wu_hbm.at[rows, :], wu.at[k], wsem.at[1, k])
        return pltpu.make_async_copy(wd_hbm.at[:, rows], wd.at[k], wsem.at[2, k])

    def remote(src, dst, ssem, rsem, to):
        return pltpu.make_async_remote_copy(
            src_ref=src, dst_ref=dst, send_sem=ssem, recv_sem=rsem,
            device_id={"expert": to}, device_id_type=MESH,
        )

    def raw_copy(k):
        return remote(own.at[k], raw.at[k], raw_s.at[k], raw_r.at[k], partner)

    def x_copy(q, k, to):
        return remote(x.at[q, k], x.at[q, k], x_s.at[q, k], x_r.at[q, k], to)

    def r_copy(q, j):
        return remote(rout.at[q, j], rin.at[q, j], r_s.at[q, j], r_r.at[q, j], me + 1)

    def l_copy(q, j):
        return remote(lout.at[q, j], lin.at[q, j], l_s.at[q, j], l_r.at[q, j], me - 1)

    barrier = pltpu.get_barrier_semaphore()

    @pl.when(has_left)
    def _():
        pl.semaphore_signal(barrier, inc=1, device_id={"expert": me - 1}, device_id_type=MESH)

    @pl.when(has_right)
    def _():
        pl.semaphore_signal(barrier, inc=1, device_id={"expert": me + 1}, device_id_type=MESH)

    @loop(0, chunks)
    def _(k):
        weight(0, k).start()
        weight(1, k).start()

    @loop(0, chunks)
    def _(k):
        weight(2, k).start()

    slot = slot_ref[...]
    routed = slot < cap
    count = jnp.sum(routed.astype(jnp.int32), axis=1, keepdims=True)
    row = slot + odd * (cap - count)
    at = lax.broadcasted_iota(jnp.int32, (cap, slot.shape[1]), 0)
    pick = (at == row) & routed
    pick_half = jnp.where(pick, 1.0, 0.0).astype(BF16)
    prob = prob_ref[...]
    share = jnp.where(ids_ref[0:1, :] == 0, prob, jnp.where(ids_ref[1:2, :] == 0, 1.0 - prob, 0.0))
    row_share = jnp.sum(jnp.where(pick, share, 0.0), axis=1, keepdims=True)

    pl.semaphore_wait(barrier, has_left.astype(jnp.int32) + has_right.astype(jnp.int32))

    for k in range(chunks):
        own[k] = jnp.dot(
            pick_half, tok_ref[:, k * width:(k + 1) * width], preferred_element_type=F32
        ).astype(BF16)
        raw_copy(k).start()

    def forwards(q):
        return ((q < pair) & has_right) | ((q > pair) & has_left)

    def forward(k):
        for q in range(pairs):
            @pl.when(forwards(q))
            def _():
                to = jnp.where(q < pair, me + 1, me - 1)
                x_copy(q, k, to).wait_recv()
                x_copy(q, k, to).start()

    def project(q, k):
        block = x[q, k]
        for t in range(0, hidden, tile):
            cols = slice(t, t + tile)
            gate = jnp.dot(block, wg[k, :, cols], preferred_element_type=F32)
            up = jnp.dot(block, wu[k, :, cols], preferred_element_type=F32)
            gacc[:, cols] += gate
            uacc[:, cols] += up

    def finish(q, first):
        for t in range(0, hidden, tile):
            cols = slice(t, t + tile)
            gate = gacc[:, cols]
            hid[:, cols] = (gate / (1.0 + jnp.exp(-gate)) * uacc[:, cols]).astype(BF16)

        @loop(0, chunks)
        def _(j):
            if first:
                weight(2, j).wait()
            value = jnp.dot(hid[...], wd[j], preferred_element_type=F32)
            part[q, j] = value

            @pl.when(me == 0)
            def _():
                rout[q, j] = value.astype(BF16)
                r_copy(q, j).start()

            @pl.when(me == n - 1)
            def _():
                lout[q, j] = value.astype(BF16)
                l_copy(q, j).start()

    gacc[...] = jnp.zeros_like(gacc)
    uacc[...] = jnp.zeros_like(uacc)

    @loop(0, chunks)
    def _(k):
        raw_copy(k).wait_recv()
        x[pair, k] = own[k] + raw[k]

        @pl.when((odd == 1) & has_right)
        def _():
            x_copy(pair, k, me + 1).start()

        @pl.when((odd == 0) & has_left)
        def _():
            x_copy(pair, k, me - 1).start()

        @pl.when(k > 0)
        def _():
            forward(k - 1)

        weight(0, k).wait()
        weight(1, k).wait()
        project(pair, k)

    forward(chunks - 1)
    finish(pair, True)

    @loop(1, pairs)
    def _(s):
        q = lax.rem(pair + s, pairs)
        gacc[...] = jnp.zeros_like(gacc)
        uacc[...] = jnp.zeros_like(uacc)

        @loop(0, chunks)
        def _(k):
            @pl.when(jnp.logical_not(forwards(q)))
            def _():
                x_copy(q, k, partner).wait_recv()

            project(q, k)

        finish(q, False)

    @loop(0, chunks)
    def _(j):
        for q in range(pairs):
            @pl.when(has_left & (me <= 2 * q))
            def _():
                r_copy(q, j).wait_recv()
                value = part[q, j] + rin[q, j].astype(F32)
                part[q, j] = value
                rout[q, j] = value.astype(BF16)
                r_copy(q, j).start()

            @pl.when(has_right & (me >= 2 * q + 1))
            def _():
                l_copy(q, j).wait_recv()
                value = part[q, j] + lin[q, j].astype(F32)
                part[q, j] = value
                lout[q, j] = value.astype(BF16)
                l_copy(q, j).start()

        def place(down):
            scaled = (row_share * down).astype(BF16)
            cols = pl.ds(pl.multiple_of(j * width, width), width)
            out_ref[:, cols] = lax.dot_general(
                pick_half, scaled, (((0,), (0,)), ((), ())), preferred_element_type=F32
            ).astype(BF16)

        @pl.when(odd == 0)
        def _():
            l_copy(pair, j).wait_recv()
            place(part[pair, j] + lin[pair, j].astype(F32))

        @pl.when(odd == 1)
        def _():
            r_copy(pair, j).wait_recv()
            place(part[pair, j] + rin[pair, j].astype(F32))

    @loop(0, chunks)
    def _(k):
        raw_copy(k).wait_send()

        @pl.when(((odd == 1) & has_right) | ((odd == 0) & has_left))
        def _():
            x_copy(pair, k, partner).wait_send()

        for q in range(pairs):
            @pl.when(forwards(q))
            def _():
                x_copy(q, k, partner).wait_send()

            @pl.when(me <= 2 * q)
            def _():
                r_copy(q, k).wait_send()

            @pl.when(me >= 2 * q + 1)
            def _():
                l_copy(q, k).wait_send()


def shards(n, tokens, w_gate, w_up, w_down, route_ids, route_prob, slot_index):
    count, model = tokens.shape
    hidden = w_gate.shape[1]
    cap = count // 2
    pairs = n // 2
    width = 512
    chunks = model // width
    flow = pltpu.VMEM((pairs, chunks, cap, width), BF16)
    dma = pltpu.SemaphoreType.DMA
    vmem = pl.BlockSpec(memory_space=pltpu.VMEM)
    hbm = pl.BlockSpec(memory_space=pl.ANY)
    return pl.pallas_call(
        functools.partial(kernel, n),
        out_shape=jax.ShapeDtypeStruct((count, model), BF16),
        in_specs=[vmem] * 4 + [hbm] * 3,
        out_specs=vmem,
        scratch_shapes=[
            pltpu.VMEM((chunks, width, hidden), BF16),
            pltpu.VMEM((chunks, width, hidden), BF16),
            pltpu.VMEM((chunks, hidden, width), BF16),
            pltpu.VMEM((chunks, cap, width), BF16),
            pltpu.VMEM((chunks, cap, width), BF16),
            flow,
            pltpu.VMEM((cap, hidden), F32),
            pltpu.VMEM((cap, hidden), F32),
            pltpu.VMEM((cap, hidden), BF16),
            pltpu.VMEM((pairs, chunks, cap, width), F32),
            flow, flow, flow, flow,
            dma((3, chunks)),
            dma((chunks,)), dma((chunks,)),
            dma((pairs, chunks)), dma((pairs, chunks)),
            dma((pairs, chunks)), dma((pairs, chunks)),
            dma((pairs, chunks)), dma((pairs, chunks)),
        ],
        compiler_params=pltpu.CompilerParams(
            collective_id=0, has_side_effects=True, vmem_limit_bytes=60 * 2**20
        ),
        cost_estimate=pl.CostEstimate(
            flops=6 * pairs * cap * model * hidden,
            bytes_accessed=6 * model * hidden,
            transcendentals=pairs * cap * hidden,
        ),
    )(slot_index[None, :], route_ids.T, route_prob[None, :], tokens, w_gate, w_up, w_down)


def solution(mesh):
    return jax.shard_map(
        functools.partial(shards, mesh.shape["expert"]),
        mesh=mesh,
        in_specs=(
            P(("dp", "expert"), None),
            P(None, "expert"),
            P(None, "expert"),
            P("expert", None),
            P(("dp", "expert"), None),
            P(("dp", "expert")),
            P(("dp", "expert")),
        ),
        out_specs=P(("dp", "expert"), None),
        check_vma=False,
    )
```

```python
import functools

import jax
import jax.numpy as jnp
from jax import lax
from jax.experimental import pallas as pl
from jax.experimental.pallas import tpu as pltpu
from jax.sharding import PartitionSpec as P

MESH = pl.DeviceIdType.MESH
F32 = jnp.float32
BF16 = jnp.bfloat16


def loop(lo, hi):
    def run(body):
        def step(i, carry):
            body(i)
            return carry

        lax.fori_loop(lo, hi, step, 0)

    return run


def kernel(
    n, slot_ref, ids_ref, prob_ref, tok_ref, wg_hbm, wu_hbm, wd_hbm, out_ref,
    wg, wu, wd, own, raw, x, gacc, uacc, hid, part, rin, lin, rout, lout,
    wsem, raw_s, raw_r, x_s, x_r, r_s, r_r, l_s, l_r,
):
    me = lax.axis_index("expert")
    chunks, cap, width = own.shape
    pairs = n // 2
    hidden = hid.shape[1]
    tile = min(512, hidden)
    ahead = min(2, chunks)
    pair = me // 2
    odd = me % 2
    partner = me + 1 - 2 * odd
    has_left, has_right = me > 0, me < n - 1

    def weight(which, k):
        rows = pl.ds(pl.multiple_of(k * width, width), width)
        if which == 0:
            return pltpu.make_async_copy(wg_hbm.at[rows, :], wg.at[k], wsem.at[0, k])
        if which == 1:
            return pltpu.make_async_copy(wu_hbm.at[rows, :], wu.at[k], wsem.at[1, k])
        return pltpu.make_async_copy(wd_hbm.at[:, rows], wd.at[k], wsem.at[2, k])

    def remote(src, dst, ssem, rsem, to):
        return pltpu.make_async_remote_copy(
            src_ref=src, dst_ref=dst, send_sem=ssem, recv_sem=rsem,
            device_id={"expert": to}, device_id_type=MESH,
        )

    def raw_copy(k):
        return remote(own.at[k], raw.at[k], raw_s.at[k], raw_r.at[k], partner)

    def rows_of(q):
        return pl.ds(pl.multiple_of(q * cap, cap), cap)

    def x_copy(q, k, to):
        block = x.at[k, rows_of(q), :]
        return remote(block, block, x_s.at[q, k], x_r.at[q, k], to)

    def r_copy(q, j):
        return remote(rout.at[q, j], rin.at[q, j], r_s.at[q, j], r_r.at[q, j], me + 1)

    def l_copy(q, j):
        return remote(lout.at[q, j], lin.at[q, j], l_s.at[q, j], l_r.at[q, j], me - 1)

    barrier = pltpu.get_barrier_semaphore()

    @pl.when(has_left)
    def _():
        pl.semaphore_signal(barrier, inc=1, device_id={"expert": me - 1}, device_id_type=MESH)

    @pl.when(has_right)
    def _():
        pl.semaphore_signal(barrier, inc=1, device_id={"expert": me + 1}, device_id_type=MESH)

    @loop(0, chunks)
    def _(k):
        weight(0, k).start()
        weight(1, k).start()

    @loop(0, chunks)
    def _(k):
        weight(2, k).start()

    slot = slot_ref[...]
    routed = slot < cap
    count = jnp.sum(routed.astype(jnp.int32), axis=1, keepdims=True)
    row = slot + odd * (cap - count)
    at = lax.broadcasted_iota(jnp.int32, (cap, slot.shape[1]), 0)
    pick = (at == row) & routed
    pick_half = jnp.where(pick, 1.0, 0.0).astype(BF16)
    prob = prob_ref[...]
    share = jnp.where(ids_ref[0:1, :] == 0, prob, jnp.where(ids_ref[1:2, :] == 0, 1.0 - prob, 0.0))
    row_share = jnp.sum(jnp.where(pick, share, 0.0), axis=1, keepdims=True)

    pl.semaphore_wait(barrier, has_left.astype(jnp.int32) + has_right.astype(jnp.int32))

    for k in range(chunks):
        own[k] = jnp.dot(
            pick_half, tok_ref[:, k * width:(k + 1) * width], preferred_element_type=F32
        ).astype(BF16)
        if k < ahead:
            raw_copy(k).start()

    def forwards(q):
        return ((q < pair) & has_right) | ((q > pair) & has_left)

    def project(k):
        for q in range(pairs):
            @pl.when(q != pair)
            def _():
                to = jnp.where(q < pair, me + 1, me - 1)
                x_copy(q, k, to).wait_recv()

                @pl.when(forwards(q))
                def _():
                    x_copy(q, k, to).start()

        weight(0, k).wait()
        weight(1, k).wait()
        block = x[k]
        for t in range(0, hidden, tile):
            cols = slice(t, t + tile)
            gacc[:, cols] += jnp.dot(block, wg[k, :, cols], preferred_element_type=F32)
            uacc[:, cols] += jnp.dot(block, wu[k, :, cols], preferred_element_type=F32)

    gacc[...] = jnp.zeros_like(gacc)
    uacc[...] = jnp.zeros_like(uacc)

    @loop(0, chunks)
    def _(k):
        raw_copy(k).wait_recv()
        x[k, rows_of(pair), :] = own[k] + raw[k]

        @pl.when((odd == 1) & has_right)
        def _():
            x_copy(pair, k, me + 1).start()

        @pl.when((odd == 0) & has_left)
        def _():
            x_copy(pair, k, me - 1).start()

        @pl.when(k + ahead < chunks)
        def _():
            raw_copy(k + ahead).start()

        @pl.when(k > 0)
        def _():
            project(k - 1)

    project(chunks - 1)

    for t in range(0, hidden, tile):
        cols = slice(t, t + tile)
        gate = gacc[:, cols]
        hid[:, cols] = (gate / (1.0 + jnp.exp(-gate)) * uacc[:, cols]).astype(BF16)

    def send_from_ends(q, j):
        @pl.when(me == 0)
        def _():
            rout[q, j] = part[j, rows_of(q), :].astype(BF16)
            r_copy(q, j).start()

        @pl.when(me == n - 1)
        def _():
            lout[q, j] = part[j, rows_of(q), :].astype(BF16)
            l_copy(q, j).start()

    @loop(0, chunks)
    def _(j):
        weight(2, j).wait()
        part[j] = jnp.dot(hid[...], wd[j], preferred_element_type=F32)
        for q in range(pairs):
            @pl.when(q != pair)
            def _():
                send_from_ends(q, j)

    @loop(0, chunks)
    def _(j):
        send_from_ends(pair, j)

    @loop(0, chunks)
    def _(j):
        for q in range(pairs):
            @pl.when(has_left & (me <= 2 * q))
            def _():
                r_copy(q, j).wait_recv()
                value = part[j, rows_of(q), :] + rin[q, j].astype(F32)
                part[j, rows_of(q), :] = value
                rout[q, j] = value.astype(BF16)
                r_copy(q, j).start()

            @pl.when(has_right & (me >= 2 * q + 1))
            def _():
                l_copy(q, j).wait_recv()
                value = part[j, rows_of(q), :] + lin[q, j].astype(F32)
                part[j, rows_of(q), :] = value
                lout[q, j] = value.astype(BF16)
                l_copy(q, j).start()

    @loop(0, chunks)
    def _(j):
        def place(other):
            down = part[j, rows_of(pair), :] + other.astype(F32)
            scaled = (row_share * down).astype(BF16)
            cols = pl.ds(pl.multiple_of(j * width, width), width)
            out_ref[:, cols] = lax.dot_general(
                pick_half, scaled, (((0,), (0,)), ((), ())), preferred_element_type=F32
            ).astype(BF16)

        @pl.when(odd == 0)
        def _():
            l_copy(pair, j).wait_recv()
            place(lin[pair, j])

        @pl.when(odd == 1)
        def _():
            r_copy(pair, j).wait_recv()
            place(rin[pair, j])

    @loop(0, chunks)
    def _(k):
        raw_copy(k).wait_send()

        @pl.when(((odd == 1) & has_right) | ((odd == 0) & has_left))
        def _():
            x_copy(pair, k, partner).wait_send()

        for q in range(pairs):
            @pl.when(forwards(q))
            def _():
                x_copy(q, k, partner).wait_send()

            @pl.when(me <= 2 * q)
            def _():
                r_copy(q, k).wait_send()

            @pl.when(me >= 2 * q + 1)
            def _():
                l_copy(q, k).wait_send()


def shards(n, tokens, w_gate, w_up, w_down, route_ids, route_prob, slot_index):
    count, model = tokens.shape
    hidden = w_gate.shape[1]
    cap = count // 2
    pairs = n // 2
    rows = pairs * cap
    width = 512
    chunks = model // width
    flow = pltpu.VMEM((pairs, chunks, cap, width), BF16)
    dma = pltpu.SemaphoreType.DMA
    vmem = pl.BlockSpec(memory_space=pltpu.VMEM)
    hbm = pl.BlockSpec(memory_space=pl.ANY)
    return pl.pallas_call(
        functools.partial(kernel, n),
        out_shape=jax.ShapeDtypeStruct((count, model), BF16),
        in_specs=[vmem] * 4 + [hbm] * 3,
        out_specs=vmem,
        scratch_shapes=[
            pltpu.VMEM((chunks, width, hidden), BF16),
            pltpu.VMEM((chunks, width, hidden), BF16),
            pltpu.VMEM((chunks, hidden, width), BF16),
            pltpu.VMEM((chunks, cap, width), BF16),
            pltpu.VMEM((chunks, cap, width), BF16),
            pltpu.VMEM((chunks, rows, width), BF16),
            pltpu.VMEM((rows, hidden), F32),
            pltpu.VMEM((rows, hidden), F32),
            pltpu.VMEM((rows, hidden), BF16),
            pltpu.VMEM((chunks, rows, width), F32),
            flow, flow, flow, flow,
            dma((3, chunks)),
            dma((chunks,)), dma((chunks,)),
            dma((pairs, chunks)), dma((pairs, chunks)),
            dma((pairs, chunks)), dma((pairs, chunks)),
            dma((pairs, chunks)), dma((pairs, chunks)),
        ],
        compiler_params=pltpu.CompilerParams(
            collective_id=0, has_side_effects=True, vmem_limit_bytes=60 * 2**20
        ),
        cost_estimate=pl.CostEstimate(
            flops=6 * pairs * cap * model * hidden,
            bytes_accessed=6 * model * hidden,
            transcendentals=pairs * cap * hidden,
        ),
    )(slot_index[None, :], route_ids.T, route_prob[None, :], tokens, w_gate, w_up, w_down)


def solution(mesh):
    return jax.shard_map(
        functools.partial(shards, mesh.shape["expert"]),
        mesh=mesh,
        in_specs=(
            P(("dp", "expert"), None),
            P(None, "expert"),
            P(None, "expert"),
            P("expert", None),
            P(("dp", "expert"), None),
            P(("dp", "expert")),
            P(("dp", "expert")),
        ),
        out_specs=P(("dp", "expert"), None),
        check_vma=False,
    )
```

```python
import functools

import jax
import jax.numpy as jnp
from jax import lax
from jax.experimental import pallas as pl
from jax.experimental.pallas import tpu as pltpu
from jax.sharding import PartitionSpec as P

MESH = pl.DeviceIdType.MESH
F32 = jnp.float32
BF16 = jnp.bfloat16


def loop(lo, hi):
    def run(body):
        def step(i, carry):
            body(i)
            return carry

        lax.fori_loop(lo, hi, step, 0)

    return run


def kernel(
    n, slot_ref, ids_ref, prob_ref, tok_ref, wg_hbm, wu_hbm, wd_hbm, out_ref,
    wg, wu, wd, own, raw, x, gacc, uacc, hid, part, rin, lin, rout, lout,
    wsem, raw_s, raw_r, x_s, x_r, r_s, r_r, l_s, l_r,
):
    me = lax.axis_index("expert")
    chunks, cap, width = own.shape
    pairs = n // 2
    hidden = hid.shape[1]
    tile = min(512, hidden)
    ahead = min(2, chunks)
    window = min(3, chunks)
    pair = me // 2
    odd = me % 2
    partner = me + 1 - 2 * odd
    has_left, has_right = me > 0, me < n - 1

    def weight(which, k):
        rows = pl.ds(pl.multiple_of(k * width, width), width)
        if which == 0:
            return pltpu.make_async_copy(wg_hbm.at[rows, :], wg.at[k], wsem.at[0, k])
        if which == 1:
            return pltpu.make_async_copy(wu_hbm.at[rows, :], wu.at[k], wsem.at[1, k])
        return pltpu.make_async_copy(wd_hbm.at[:, rows], wd.at[k], wsem.at[2, k])

    def remote(src, dst, ssem, rsem, to):
        return pltpu.make_async_remote_copy(
            src_ref=src, dst_ref=dst, send_sem=ssem, recv_sem=rsem,
            device_id={"expert": to}, device_id_type=MESH,
        )

    def raw_copy(k):
        return remote(own.at[k], raw.at[k], raw_s.at[k], raw_r.at[k], partner)

    def rows_of(q):
        return pl.ds(pl.multiple_of(q * cap, cap), cap)

    def x_copy(q, k, to):
        block = x.at[k, rows_of(q), :]
        return remote(block, block, x_s.at[q, k], x_r.at[q, k], to)

    def r_copy(q, j):
        return remote(rout.at[q, j], rin.at[q, j], r_s.at[q, j], r_r.at[q, j], me + 1)

    def l_copy(q, j):
        return remote(lout.at[q, j], lin.at[q, j], l_s.at[q, j], l_r.at[q, j], me - 1)

    barrier = pltpu.get_barrier_semaphore()

    @pl.when(has_left)
    def _():
        pl.semaphore_signal(barrier, inc=1, device_id={"expert": me - 1}, device_id_type=MESH)

    @pl.when(has_right)
    def _():
        pl.semaphore_signal(barrier, inc=1, device_id={"expert": me + 1}, device_id_type=MESH)

    slot = slot_ref[...]
    routed = slot < cap
    count = jnp.sum(routed.astype(jnp.int32), axis=1, keepdims=True)
    row = slot + odd * (cap - count)
    at = lax.broadcasted_iota(jnp.int32, (cap, slot.shape[1]), 0)
    pick = (at == row) & routed
    pick_half = jnp.where(pick, 1.0, 0.0).astype(BF16)
    prob = prob_ref[...]
    share = jnp.where(ids_ref[0:1, :] == 0, prob, jnp.where(ids_ref[1:2, :] == 0, 1.0 - prob, 0.0))
    row_share = jnp.sum(jnp.where(pick, share, 0.0), axis=1, keepdims=True)

    pl.semaphore_wait(barrier, has_left.astype(jnp.int32) + has_right.astype(jnp.int32))

    for k in range(chunks):
        own[k] = jnp.dot(
            pick_half, tok_ref[:, k * width:(k + 1) * width], preferred_element_type=F32
        ).astype(BF16)
        if k < ahead:
            raw_copy(k).start()

    for k in range(window):
        weight(0, k).start()
        weight(1, k).start()

    def forwards(q):
        return ((q < pair) & has_right) | ((q > pair) & has_left)

    def project(k):
        for q in range(pairs):
            @pl.when(q != pair)
            def _():
                to = jnp.where(q < pair, me + 1, me - 1)
                x_copy(q, k, to).wait_recv()

                @pl.when(forwards(q))
                def _():
                    x_copy(q, k, to).start()

        weight(0, k).wait()
        weight(1, k).wait()

        @pl.when(k + window < chunks)
        def _():
            weight(0, k + window).start()
            weight(1, k + window).start()

        @pl.when(k + window >= chunks)
        def _():
            weight(2, k + window - chunks).start()

        block = x[k]
        for t in range(0, hidden, tile):
            cols = slice(t, t + tile)
            gacc[:, cols] += jnp.dot(block, wg[k, :, cols], preferred_element_type=F32)
            uacc[:, cols] += jnp.dot(block, wu[k, :, cols], preferred_element_type=F32)

    gacc[...] = jnp.zeros_like(gacc)
    uacc[...] = jnp.zeros_like(uacc)

    @loop(0, chunks)
    def _(k):
        raw_copy(k).wait_recv()
        x[k, rows_of(pair), :] = own[k] + raw[k]

        @pl.when((odd == 1) & has_right)
        def _():
            x_copy(pair, k, me + 1).start()

        @pl.when((odd == 0) & has_left)
        def _():
            x_copy(pair, k, me - 1).start()

        @pl.when(k + ahead < chunks)
        def _():
            raw_copy(k + ahead).start()

        @pl.when(k > 0)
        def _():
            project(k - 1)

    project(jnp.int32(chunks - 1))

    for t in range(0, hidden, tile):
        cols = slice(t, t + tile)
        gate = gacc[:, cols]
        hid[:, cols] = (gate / (1.0 + jnp.exp(-gate)) * uacc[:, cols]).astype(BF16)

    def send_from_ends(q, j):
        @pl.when(me == 0)
        def _():
            rout[q, j] = part[j, rows_of(q), :].astype(BF16)
            r_copy(q, j).start()

        @pl.when(me == n - 1)
        def _():
            lout[q, j] = part[j, rows_of(q), :].astype(BF16)
            l_copy(q, j).start()

    @loop(0, chunks)
    def _(j):
        weight(2, j).wait()

        @pl.when(j + window < chunks)
        def _():
            weight(2, j + window).start()

        part[j] = jnp.dot(hid[...], wd[j], preferred_element_type=F32)
        for q in range(pairs):
            @pl.when(q != pair)
            def _():
                send_from_ends(q, j)

    @loop(0, chunks)
    def _(j):
        send_from_ends(pair, j)

    @loop(0, chunks)
    def _(j):
        for q in range(pairs):
            @pl.when(has_left & (me <= 2 * q))
            def _():
                r_copy(q, j).wait_recv()
                value = part[j, rows_of(q), :] + rin[q, j].astype(F32)
                part[j, rows_of(q), :] = value
                rout[q, j] = value.astype(BF16)
                r_copy(q, j).start()

            @pl.when(has_right & (me >= 2 * q + 1))
            def _():
                l_copy(q, j).wait_recv()
                value = part[j, rows_of(q), :] + lin[q, j].astype(F32)
                part[j, rows_of(q), :] = value
                lout[q, j] = value.astype(BF16)
                l_copy(q, j).start()

    @loop(0, chunks)
    def _(j):
        def place(other):
            down = part[j, rows_of(pair), :] + other.astype(F32)
            scaled = (row_share * down).astype(BF16)
            cols = pl.ds(pl.multiple_of(j * width, width), width)
            out_ref[:, cols] = lax.dot_general(
                pick_half, scaled, (((0,), (0,)), ((), ())), preferred_element_type=F32
            ).astype(BF16)

        @pl.when(odd == 0)
        def _():
            l_copy(pair, j).wait_recv()
            place(lin[pair, j])

        @pl.when(odd == 1)
        def _():
            r_copy(pair, j).wait_recv()
            place(rin[pair, j])

    @loop(0, chunks)
    def _(k):
        raw_copy(k).wait_send()

        @pl.when(((odd == 1) & has_right) | ((odd == 0) & has_left))
        def _():
            x_copy(pair, k, partner).wait_send()

        for q in range(pairs):
            @pl.when(forwards(q))
            def _():
                x_copy(q, k, partner).wait_send()

            @pl.when(me <= 2 * q)
            def _():
                r_copy(q, k).wait_send()

            @pl.when(me >= 2 * q + 1)
            def _():
                l_copy(q, k).wait_send()


def shards(n, tokens, w_gate, w_up, w_down, route_ids, route_prob, slot_index):
    count, model = tokens.shape
    hidden = w_gate.shape[1]
    cap = count // 2
    pairs = n // 2
    rows = pairs * cap
    width = 512
    chunks = model // width
    flow = pltpu.VMEM((pairs, chunks, cap, width), BF16)
    dma = pltpu.SemaphoreType.DMA
    vmem = pl.BlockSpec(memory_space=pltpu.VMEM)
    hbm = pl.BlockSpec(memory_space=pl.ANY)
    return pl.pallas_call(
        functools.partial(kernel, n),
        out_shape=jax.ShapeDtypeStruct((count, model), BF16),
        in_specs=[vmem] * 4 + [hbm] * 3,
        out_specs=vmem,
        scratch_shapes=[
            pltpu.VMEM((chunks, width, hidden), BF16),
            pltpu.VMEM((chunks, width, hidden), BF16),
            pltpu.VMEM((chunks, hidden, width), BF16),
            pltpu.VMEM((chunks, cap, width), BF16),
            pltpu.VMEM((chunks, cap, width), BF16),
            pltpu.VMEM((chunks, rows, width), BF16),
            pltpu.VMEM((rows, hidden), F32),
            pltpu.VMEM((rows, hidden), F32),
            pltpu.VMEM((rows, hidden), BF16),
            pltpu.VMEM((chunks, rows, width), F32),
            flow, flow, flow, flow,
            dma((3, chunks)),
            dma((chunks,)), dma((chunks,)),
            dma((pairs, chunks)), dma((pairs, chunks)),
            dma((pairs, chunks)), dma((pairs, chunks)),
            dma((pairs, chunks)), dma((pairs, chunks)),
        ],
        compiler_params=pltpu.CompilerParams(
            collective_id=0, has_side_effects=True, vmem_limit_bytes=60 * 2**20
        ),
        cost_estimate=pl.CostEstimate(
            flops=6 * pairs * cap * model * hidden,
            bytes_accessed=6 * model * hidden,
            transcendentals=pairs * cap * hidden,
        ),
    )(slot_index[None, :], route_ids.T, route_prob[None, :], tokens, w_gate, w_up, w_down)


def solution(mesh):
    return jax.shard_map(
        functools.partial(shards, mesh.shape["expert"]),
        mesh=mesh,
        in_specs=(
            P(("dp", "expert"), None),
            P(None, "expert"),
            P(None, "expert"),
            P("expert", None),
            P(("dp", "expert"), None),
            P(("dp", "expert")),
            P(("dp", "expert")),
        ),
        out_specs=P(("dp", "expert"), None),
        check_vma=False,
    )
```

```python
import functools

import jax
import jax.numpy as jnp
from jax import lax
from jax.experimental import pallas as pl
from jax.experimental.pallas import tpu as pltpu
from jax.sharding import PartitionSpec as P

MESH = pl.DeviceIdType.MESH
F32 = jnp.float32
BF16 = jnp.bfloat16


def loop(lo, hi):
    def run(body):
        def step(i, carry):
            body(i)
            return carry

        lax.fori_loop(lo, hi, step, 0)

    return run


def kernel(
    n, slot_ref, ids_ref, prob_ref, tok_ref, wg_hbm, wu_hbm, wd_hbm, out_ref,
    wg, wu, wd, own, raw, x, gacc, uacc, hid, part, rin, lin, rout, lout,
    wsem, raw_s, raw_r, x_s, x_r, r_s, r_r, l_s, l_r,
):
    me = lax.axis_index("expert")
    chunks, cap, width = own.shape
    pairs = n // 2
    hidden = hid.shape[1]
    tile = min(512, hidden)
    pair = me // 2
    odd = me % 2
    partner = me + 1 - 2 * odd
    has_left, has_right = me > 0, me < n - 1

    def weight(which, k):
        rows = pl.ds(pl.multiple_of(k * width, width), width)
        if which == 0:
            return pltpu.make_async_copy(wg_hbm.at[rows, :], wg.at[k], wsem.at[0, k])
        if which == 1:
            return pltpu.make_async_copy(wu_hbm.at[rows, :], wu.at[k], wsem.at[1, k])
        return pltpu.make_async_copy(wd_hbm.at[:, rows], wd.at[k], wsem.at[2, k])

    def remote(src, dst, ssem, rsem, to):
        return pltpu.make_async_remote_copy(
            src_ref=src, dst_ref=dst, send_sem=ssem, recv_sem=rsem,
            device_id={"expert": to}, device_id_type=MESH,
        )

    def raw_copy(k):
        return remote(own.at[k], raw.at[k], raw_s.at[k], raw_r.at[k], partner)

    def rows_of(q):
        return pl.ds(pl.multiple_of(q * cap, cap), cap)

    def x_copy(q, k, to):
        block = x.at[k, rows_of(q), :]
        return remote(block, block, x_s.at[q, k], x_r.at[q, k], to)

    def r_copy(q, j):
        return remote(rout.at[q, j], rin.at[q, j], r_s.at[q, j], r_r.at[q, j], me + 1)

    def l_copy(q, j):
        return remote(lout.at[q, j], lin.at[q, j], l_s.at[q, j], l_r.at[q, j], me - 1)

    barrier = pltpu.get_barrier_semaphore()

    @pl.when(has_left)
    def _():
        pl.semaphore_signal(barrier, inc=1, device_id={"expert": me - 1}, device_id_type=MESH)

    @pl.when(has_right)
    def _():
        pl.semaphore_signal(barrier, inc=1, device_id={"expert": me + 1}, device_id_type=MESH)

    slot = slot_ref[...]
    routed = slot < cap
    count = jnp.sum(routed.astype(jnp.int32), axis=1, keepdims=True)
    row = slot + odd * (cap - count)
    at = lax.broadcasted_iota(jnp.int32, (cap, slot.shape[1]), 0)
    pick = (at == row) & routed
    pick_half = jnp.where(pick, 1.0, 0.0).astype(BF16)
    prob = prob_ref[...]
    share = jnp.where(ids_ref[0:1, :] == 0, prob, jnp.where(ids_ref[1:2, :] == 0, 1.0 - prob, 0.0))
    row_share = jnp.sum(jnp.where(pick, share, 0.0), axis=1, keepdims=True)

    pl.semaphore_wait(barrier, has_left.astype(jnp.int32) + has_right.astype(jnp.int32))

    for k in range(chunks):
        own[k] = jnp.dot(
            pick_half, tok_ref[:, k * width:(k + 1) * width], preferred_element_type=F32
        ).astype(BF16)
        raw_copy(k).start()

    @loop(0, chunks)
    def _(k):
        weight(0, k).start()
        weight(1, k).start()

    @loop(0, chunks)
    def _(k):
        weight(2, k).start()

    def forwards(q):
        return ((q < pair) & has_right) | ((q > pair) & has_left)

    def forward(k):
        for q in range(pairs):
            @pl.when(forwards(q))
            def _():
                x_copy(q, k, partner).wait_recv()
                x_copy(q, k, jnp.where(q < pair, me + 1, me - 1)).start()

    @loop(0, chunks)
    def _(k):
        raw_copy(k).wait_recv()
        x[k, rows_of(pair), :] = own[k] + raw[k]

        @pl.when((odd == 1) & has_right)
        def _():
            x_copy(pair, k, me + 1).start()

        @pl.when((odd == 0) & has_left)
        def _():
            x_copy(pair, k, me - 1).start()

        @pl.when(k > 0)
        def _():
            forward(k - 1)

    forward(chunks - 1)

    gacc[...] = jnp.zeros_like(gacc)
    uacc[...] = jnp.zeros_like(uacc)

    @loop(0, chunks)
    def _(k):
        for q in range(pairs):
            @pl.when((q != pair) & jnp.logical_not(forwards(q)))
            def _():
                x_copy(q, k, partner).wait_recv()

        weight(0, k).wait()
        weight(1, k).wait()
        block = x[k]
        for t in range(0, hidden, tile):
            cols = slice(t, t + tile)
            gacc[:, cols] += jnp.dot(block, wg[k, :, cols], preferred_element_type=F32)
            uacc[:, cols] += jnp.dot(block, wu[k, :, cols], preferred_element_type=F32)

    for t in range(0, hidden, tile):
        cols = slice(t, t + tile)
        gate = gacc[:, cols]
        hid[:, cols] = (gate / (1.0 + jnp.exp(-gate)) * uacc[:, cols]).astype(BF16)

    def send_from_ends(q, j):
        @pl.when(me == 0)
        def _():
            rout[q, j] = part[j, rows_of(q), :].astype(BF16)
            r_copy(q, j).start()

        @pl.when(me == n - 1)
        def _():
            lout[q, j] = part[j, rows_of(q), :].astype(BF16)
            l_copy(q, j).start()

    @loop(0, chunks)
    def _(j):
        weight(2, j).wait()
        part[j] = jnp.dot(hid[...], wd[j], preferred_element_type=F32)
        for q in range(pairs):
            @pl.when(q != pair)
            def _():
                send_from_ends(q, j)

    @loop(0, chunks)
    def _(j):
        send_from_ends(pair, j)

    @loop(0, chunks)
    def _(j):
        for q in range(pairs):
            @pl.when(has_left & (me <= 2 * q))
            def _():
                r_copy(q, j).wait_recv()
                value = part[j, rows_of(q), :] + rin[q, j].astype(F32)
                part[j, rows_of(q), :] = value
                rout[q, j] = value.astype(BF16)
                r_copy(q, j).start()

            @pl.when(has_right & (me >= 2 * q + 1))
            def _():
                l_copy(q, j).wait_recv()
                value = part[j, rows_of(q), :] + lin[q, j].astype(F32)
                part[j, rows_of(q), :] = value
                lout[q, j] = value.astype(BF16)
                l_copy(q, j).start()

    @loop(0, chunks)
    def _(j):
        def place(other):
            down = part[j, rows_of(pair), :] + other.astype(F32)
            scaled = (row_share * down).astype(BF16)
            cols = pl.ds(pl.multiple_of(j * width, width), width)
            out_ref[:, cols] = lax.dot_general(
                pick_half, scaled, (((0,), (0,)), ((), ())), preferred_element_type=F32
            ).astype(BF16)

        @pl.when(odd == 0)
        def _():
            l_copy(pair, j).wait_recv()
            place(lin[pair, j])

        @pl.when(odd == 1)
        def _():
            r_copy(pair, j).wait_recv()
            place(rin[pair, j])

    @loop(0, chunks)
    def _(k):
        raw_copy(k).wait_send()

        @pl.when(((odd == 1) & has_right) | ((odd == 0) & has_left))
        def _():
            x_copy(pair, k, partner).wait_send()

        for q in range(pairs):
            @pl.when(forwards(q))
            def _():
                x_copy(q, k, partner).wait_send()

            @pl.when(me <= 2 * q)
            def _():
                r_copy(q, k).wait_send()

            @pl.when(me >= 2 * q + 1)
            def _():
                l_copy(q, k).wait_send()


def shards(n, tokens, w_gate, w_up, w_down, route_ids, route_prob, slot_index):
    count, model = tokens.shape
    hidden = w_gate.shape[1]
    cap = count // 2
    pairs = n // 2
    rows = pairs * cap
    width = 512
    chunks = model // width
    flow = pltpu.VMEM((pairs, chunks, cap, width), BF16)
    dma = pltpu.SemaphoreType.DMA
    vmem = pl.BlockSpec(memory_space=pltpu.VMEM)
    hbm = pl.BlockSpec(memory_space=pl.ANY)
    return pl.pallas_call(
        functools.partial(kernel, n),
        out_shape=jax.ShapeDtypeStruct((count, model), BF16),
        in_specs=[vmem] * 4 + [hbm] * 3,
        out_specs=vmem,
        scratch_shapes=[
            pltpu.VMEM((chunks, width, hidden), BF16),
            pltpu.VMEM((chunks, width, hidden), BF16),
            pltpu.VMEM((chunks, hidden, width), BF16),
            pltpu.VMEM((chunks, cap, width), BF16),
            pltpu.VMEM((chunks, cap, width), BF16),
            pltpu.VMEM((chunks, rows, width), BF16),
            pltpu.VMEM((rows, hidden), F32),
            pltpu.VMEM((rows, hidden), F32),
            pltpu.VMEM((rows, hidden), BF16),
            pltpu.VMEM((chunks, rows, width), F32),
            flow, flow, flow, flow,
            dma((3, chunks)),
            dma((chunks,)), dma((chunks,)),
            dma((pairs, chunks)), dma((pairs, chunks)),
            dma((pairs, chunks)), dma((pairs, chunks)),
            dma((pairs, chunks)), dma((pairs, chunks)),
        ],
        compiler_params=pltpu.CompilerParams(
            collective_id=0, has_side_effects=True, vmem_limit_bytes=60 * 2**20
        ),
        cost_estimate=pl.CostEstimate(
            flops=6 * pairs * cap * model * hidden,
            bytes_accessed=6 * model * hidden,
            transcendentals=pairs * cap * hidden,
        ),
    )(slot_index[None, :], route_ids.T, route_prob[None, :], tokens, w_gate, w_up, w_down)


def solution(mesh):
    return jax.shard_map(
        functools.partial(shards, mesh.shape["expert"]),
        mesh=mesh,
        in_specs=(
            P(("dp", "expert"), None),
            P(None, "expert"),
            P(None, "expert"),
            P("expert", None),
            P(("dp", "expert"), None),
            P(("dp", "expert")),
            P(("dp", "expert")),
        ),
        out_specs=P(("dp", "expert"), None),
        check_vma=False,
    )
```

```python
import functools

import jax
import jax.numpy as jnp
from jax import lax
from jax.experimental import pallas as pl
from jax.experimental.pallas import tpu as pltpu
from jax.sharding import PartitionSpec as P

MESH = pl.DeviceIdType.MESH
F32 = jnp.float32
BF16 = jnp.bfloat16


def loop(lo, hi):
    def run(body):
        def step(i, carry):
            body(i)
            return carry

        lax.fori_loop(lo, hi, step, 0)

    return run


def kernel(
    n, slot_ref, ids_ref, prob_ref, tok_ref, wg_hbm, wu_hbm, wd_hbm, out_ref,
    wg, wu, wd, own, raw, x, gacc, uacc, hid, part, rin, lin, rout, lout,
    wsem, raw_s, raw_r, x_s, x_r, r_s, r_r, l_s, l_r,
):
    me = lax.axis_index("expert")
    chunks, cap, width = own.shape
    pairs = n // 2
    hidden = hid.shape[1]
    tile = min(512, hidden)
    pair = me // 2
    odd = me % 2
    partner = me + 1 - 2 * odd
    has_left, has_right = me > 0, me < n - 1

    def weight(which, k):
        rows = pl.ds(pl.multiple_of(k * width, width), width)
        if which == 0:
            return pltpu.make_async_copy(wg_hbm.at[rows, :], wg.at[k], wsem.at[0, k])
        if which == 1:
            return pltpu.make_async_copy(wu_hbm.at[rows, :], wu.at[k], wsem.at[1, k])
        return pltpu.make_async_copy(wd_hbm.at[:, rows], wd.at[k], wsem.at[2, k])

    def remote(src, dst, ssem, rsem, to):
        return pltpu.make_async_remote_copy(
            src_ref=src, dst_ref=dst, send_sem=ssem, recv_sem=rsem,
            device_id={"expert": to}, device_id_type=MESH,
        )

    def raw_copy(k):
        return remote(own.at[k], raw.at[k], raw_s.at[k], raw_r.at[k], partner)

    def rows_of(q):
        return pl.ds(pl.multiple_of(q * cap, cap), cap)

    def x_copy(q, k, to):
        block = x.at[k, rows_of(q), :]
        return remote(block, block, x_s.at[q, k], x_r.at[q, k], to)

    def r_copy(q, j):
        return remote(rout.at[q, j], rin.at[q, j], r_s.at[q, j], r_r.at[q, j], me + 1)

    def l_copy(q, j):
        return remote(lout.at[q, j], lin.at[q, j], l_s.at[q, j], l_r.at[q, j], me - 1)

    barrier = pltpu.get_barrier_semaphore()

    @pl.when(has_left)
    def _():
        pl.semaphore_signal(barrier, inc=1, device_id={"expert": me - 1}, device_id_type=MESH)

    @pl.when(has_right)
    def _():
        pl.semaphore_signal(barrier, inc=1, device_id={"expert": me + 1}, device_id_type=MESH)

    slot = slot_ref[...]
    routed = slot < cap
    count = jnp.sum(routed.astype(jnp.int32), axis=1, keepdims=True)
    row = slot + odd * (cap - count)
    at = lax.broadcasted_iota(jnp.int32, (cap, slot.shape[1]), 0)
    pick = (at == row) & routed
    pick_half = jnp.where(pick, 1.0, 0.0).astype(BF16)
    prob = prob_ref[...]
    share = jnp.where(ids_ref[0:1, :] == 0, prob, jnp.where(ids_ref[1:2, :] == 0, 1.0 - prob, 0.0))
    row_share = jnp.sum(jnp.where(pick, share, 0.0), axis=1, keepdims=True)

    pl.semaphore_wait(barrier, has_left.astype(jnp.int32) + has_right.astype(jnp.int32))

    for k in range(chunks):
        own[k] = jnp.dot(
            pick_half, tok_ref[:, k * width:(k + 1) * width], preferred_element_type=F32
        ).astype(BF16)
        raw_copy(k).start()

    @loop(0, chunks)
    def _(k):
        weight(0, k).start()
        weight(1, k).start()

    @loop(0, chunks)
    def _(k):
        weight(2, k).start()

    def forwards(q):
        return ((q < pair) & has_right) | ((q > pair) & has_left)

    def forward(k):
        for q in range(pairs):
            @pl.when(forwards(q))
            def _():
                x_copy(q, k, partner).wait_recv()
                x_copy(q, k, jnp.where(q < pair, me + 1, me - 1)).start()

    @loop(0, chunks)
    def _(k):
        raw_copy(k).wait_recv()
        x[k, rows_of(pair), :] = own[k] + raw[k]

        @pl.when((odd == 1) & has_right)
        def _():
            x_copy(pair, k, me + 1).start()

        @pl.when((odd == 0) & has_left)
        def _():
            x_copy(pair, k, me - 1).start()

        @pl.when(k > 0)
        def _():
            forward(k - 1)

    forward(chunks - 1)

    def send_from_ends(q, j):
        @pl.when(me == 0)
        def _():
            rout[q, j] = part[j, rows_of(q), :].astype(BF16)
            r_copy(q, j).start()

        @pl.when(me == n - 1)
        def _():
            lout[q, j] = part[j, rows_of(q), :].astype(BF16)
            l_copy(q, j).start()

    @loop(0, pairs)
    def _(step):
        q = lax.rem(pair + step, pairs)
        gacc[...] = jnp.zeros_like(gacc)
        uacc[...] = jnp.zeros_like(uacc)

        @loop(0, chunks)
        def _(k):
            @pl.when((step > 0) & jnp.logical_not(forwards(q)))
            def _():
                x_copy(q, k, partner).wait_recv()

            @pl.when(step == 0)
            def _():
                weight(0, k).wait()
                weight(1, k).wait()

            block = x[k, rows_of(q), :]
            for t in range(0, hidden, tile):
                cols = slice(t, t + tile)
                gacc[:, cols] += jnp.dot(block, wg[k, :, cols], preferred_element_type=F32)
                uacc[:, cols] += jnp.dot(block, wu[k, :, cols], preferred_element_type=F32)

        for t in range(0, hidden, tile):
            cols = slice(t, t + tile)
            gate = gacc[:, cols]
            hid[:, cols] = (gate / (1.0 + jnp.exp(-gate)) * uacc[:, cols]).astype(BF16)

        @loop(0, chunks)
        def _(j):
            @pl.when(step == 0)
            def _():
                weight(2, j).wait()

            part[j, rows_of(q), :] = jnp.dot(hid[...], wd[j], preferred_element_type=F32)
            send_from_ends(q, j)

    @loop(0, chunks)
    def _(j):
        for q in range(pairs):
            @pl.when(has_left & (me <= 2 * q))
            def _():
                r_copy(q, j).wait_recv()
                value = part[j, rows_of(q), :] + rin[q, j].astype(F32)
                part[j, rows_of(q), :] = value
                rout[q, j] = value.astype(BF16)
                r_copy(q, j).start()

            @pl.when(has_right & (me >= 2 * q + 1))
            def _():
                l_copy(q, j).wait_recv()
                value = part[j, rows_of(q), :] + lin[q, j].astype(F32)
                part[j, rows_of(q), :] = value
                lout[q, j] = value.astype(BF16)
                l_copy(q, j).start()

    @loop(0, chunks)
    def _(j):
        def place(other):
            down = part[j, rows_of(pair), :] + other.astype(F32)
            scaled = (row_share * down).astype(BF16)
            cols = pl.ds(pl.multiple_of(j * width, width), width)
            out_ref[:, cols] = lax.dot_general(
                pick_half, scaled, (((0,), (0,)), ((), ())), preferred_element_type=F32
            ).astype(BF16)

        @pl.when(odd == 0)
        def _():
            l_copy(pair, j).wait_recv()
            place(lin[pair, j])

        @pl.when(odd == 1)
        def _():
            r_copy(pair, j).wait_recv()
            place(rin[pair, j])

    @loop(0, chunks)
    def _(k):
        raw_copy(k).wait_send()

        @pl.when(((odd == 1) & has_right) | ((odd == 0) & has_left))
        def _():
            x_copy(pair, k, partner).wait_send()

        for q in range(pairs):
            @pl.when(forwards(q))
            def _():
                x_copy(q, k, partner).wait_send()

            @pl.when(me <= 2 * q)
            def _():
                r_copy(q, k).wait_send()

            @pl.when(me >= 2 * q + 1)
            def _():
                l_copy(q, k).wait_send()


def shards(n, tokens, w_gate, w_up, w_down, route_ids, route_prob, slot_index):
    count, model = tokens.shape
    hidden = w_gate.shape[1]
    cap = count // 2
    pairs = n // 2
    rows = pairs * cap
    width = 512
    chunks = model // width
    flow = pltpu.VMEM((pairs, chunks, cap, width), BF16)
    dma = pltpu.SemaphoreType.DMA
    vmem = pl.BlockSpec(memory_space=pltpu.VMEM)
    hbm = pl.BlockSpec(memory_space=pl.ANY)
    return pl.pallas_call(
        functools.partial(kernel, n),
        out_shape=jax.ShapeDtypeStruct((count, model), BF16),
        in_specs=[vmem] * 4 + [hbm] * 3,
        out_specs=vmem,
        scratch_shapes=[
            pltpu.VMEM((chunks, width, hidden), BF16),
            pltpu.VMEM((chunks, width, hidden), BF16),
            pltpu.VMEM((chunks, hidden, width), BF16),
            pltpu.VMEM((chunks, cap, width), BF16),
            pltpu.VMEM((chunks, cap, width), BF16),
            pltpu.VMEM((chunks, rows, width), BF16),
            pltpu.VMEM((cap, hidden), F32),
            pltpu.VMEM((cap, hidden), F32),
            pltpu.VMEM((cap, hidden), BF16),
            pltpu.VMEM((chunks, rows, width), F32),
            flow, flow, flow, flow,
            dma((3, chunks)),
            dma((chunks,)), dma((chunks,)),
            dma((pairs, chunks)), dma((pairs, chunks)),
            dma((pairs, chunks)), dma((pairs, chunks)),
            dma((pairs, chunks)), dma((pairs, chunks)),
        ],
        compiler_params=pltpu.CompilerParams(
            collective_id=0, has_side_effects=True, vmem_limit_bytes=60 * 2**20
        ),
        cost_estimate=pl.CostEstimate(
            flops=6 * pairs * cap * model * hidden,
            bytes_accessed=6 * model * hidden,
            transcendentals=pairs * cap * hidden,
        ),
    )(slot_index[None, :], route_ids.T, route_prob[None, :], tokens, w_gate, w_up, w_down)


def solution(mesh):
    return jax.shard_map(
        functools.partial(shards, mesh.shape["expert"]),
        mesh=mesh,
        in_specs=(
            P(("dp", "expert"), None),
            P(None, "expert"),
            P(None, "expert"),
            P("expert", None),
            P(("dp", "expert"), None),
            P(("dp", "expert")),
            P(("dp", "expert")),
        ),
        out_specs=P(("dp", "expert"), None),
        check_vma=False,
    )
```

```python
import functools

import jax
import jax.numpy as jnp
from jax import lax
from jax.experimental import pallas as pl
from jax.experimental.pallas import tpu as pltpu
from jax.sharding import PartitionSpec as P

MESH = pl.DeviceIdType.MESH
F32 = jnp.float32
BF16 = jnp.bfloat16


def loop(lo, hi):
    def run(body):
        def step(i, carry):
            body(i)
            return carry

        lax.fori_loop(lo, hi, step, 0)

    return run


def kernel(
    n, slot_ref, ids_ref, prob_ref, tok_ref, wg_hbm, wu_hbm, wd_hbm, out_ref,
    wg, wu, wd, own, raw, x, gacc, uacc, hid, part, rin, lin, rout, lout,
    wsem, raw_s, raw_r, x_s, x_r, r_s, r_r, l_s, l_r,
):
    me = lax.axis_index("expert")
    chunks, cap, width = own.shape
    pairs = n // 2
    hidden = hid.shape[1]
    tile = min(256, hidden)
    group = 2 if chunks % 2 == 0 else 1
    pair = me // 2
    odd = me % 2
    partner = me + 1 - 2 * odd
    has_left, has_right = me > 0, me < n - 1

    def weight(which, k):
        rows = pl.ds(pl.multiple_of(k * width, width), width)
        if which == 0:
            return pltpu.make_async_copy(wg_hbm.at[rows, :], wg.at[k], wsem.at[0, k])
        if which == 1:
            return pltpu.make_async_copy(wu_hbm.at[rows, :], wu.at[k], wsem.at[1, k])
        return pltpu.make_async_copy(wd_hbm.at[:, rows], wd.at[k], wsem.at[2, k])

    def remote(src, dst, ssem, rsem, to):
        return pltpu.make_async_remote_copy(
            src_ref=src, dst_ref=dst, send_sem=ssem, recv_sem=rsem,
            device_id={"expert": to}, device_id_type=MESH,
        )

    def raw_copy(k):
        return remote(own.at[k], raw.at[k], raw_s.at[k], raw_r.at[k], partner)

    def rows_of(q):
        return pl.ds(pl.multiple_of(q * cap, cap), cap)

    def x_copy(q, k, to):
        block = x.at[k, rows_of(q), :]
        return remote(block, block, x_s.at[q, k], x_r.at[q, k], to)

    def r_copy(q, j):
        return remote(rout.at[q, j], rin.at[q, j], r_s.at[q, j], r_r.at[q, j], me + 1)

    def l_copy(q, j):
        return remote(lout.at[q, j], lin.at[q, j], l_s.at[q, j], l_r.at[q, j], me - 1)

    barrier = pltpu.get_barrier_semaphore()

    @pl.when(has_left)
    def _():
        pl.semaphore_signal(barrier, inc=1, device_id={"expert": me - 1}, device_id_type=MESH)

    @pl.when(has_right)
    def _():
        pl.semaphore_signal(barrier, inc=1, device_id={"expert": me + 1}, device_id_type=MESH)

    slot = slot_ref[...]
    routed = slot < cap
    count = jnp.sum(routed.astype(jnp.int32), axis=1, keepdims=True)
    row = slot + odd * (cap - count)
    at = lax.broadcasted_iota(jnp.int32, (cap, slot.shape[1]), 0)
    pick = (at == row) & routed
    pick_half = jnp.where(pick, 1.0, 0.0).astype(BF16)
    prob = prob_ref[...]
    share = jnp.where(ids_ref[0:1, :] == 0, prob, jnp.where(ids_ref[1:2, :] == 0, 1.0 - prob, 0.0))
    row_share = jnp.sum(jnp.where(pick, share, 0.0), axis=1, keepdims=True)

    pl.semaphore_wait(barrier, has_left.astype(jnp.int32) + has_right.astype(jnp.int32))

    for k in range(chunks):
        own[k] = jnp.dot(
            pick_half, tok_ref[:, k * width:(k + 1) * width], preferred_element_type=F32
        ).astype(BF16)
        raw_copy(k).start()

    @loop(0, chunks)
    def _(k):
        weight(0, k).start()
        weight(1, k).start()

    @loop(0, chunks)
    def _(k):
        weight(2, k).start()

    def forwards(q):
        return ((q < pair) & has_right) | ((q > pair) & has_left)

    def forward(k):
        for q in range(pairs):
            @pl.when(forwards(q))
            def _():
                x_copy(q, k, partner).wait_recv()
                x_copy(q, k, jnp.where(q < pair, me + 1, me - 1)).start()

    @loop(0, chunks)
    def _(k):
        raw_copy(k).wait_recv()
        x[k, rows_of(pair), :] = own[k] + raw[k]

        @pl.when((odd == 1) & has_right)
        def _():
            x_copy(pair, k, me + 1).start()

        @pl.when((odd == 0) & has_left)
        def _():
            x_copy(pair, k, me - 1).start()

        @pl.when(k > 0)
        def _():
            forward(k - 1)

    forward(chunks - 1)

    def project(first, fresh):
        taken = [first + i for i in range(group)]
        for k in taken:
            for q in range(pairs):
                @pl.when((q != pair) & jnp.logical_not(forwards(q)))
                def _():
                    x_copy(q, k, partner).wait_recv()

            weight(0, k).wait()
            weight(1, k).wait()
        for t in range(0, hidden, tile):
            cols = slice(t, t + tile)
            for total, w in ((gacc, wg), (uacc, wu)):
                value = None if fresh else total[:, cols]
                for k in taken:
                    term = jnp.dot(x[k], w[k, :, cols], preferred_element_type=F32)
                    value = term if value is None else value + term
                total[:, cols] = value

    project(0, True)

    @loop(1, chunks // group)
    def _(g):
        project(g * group, False)

    for t in range(0, hidden, tile):
        cols = slice(t, t + tile)
        gate = gacc[:, cols]
        hid[:, cols] = (gate / (1.0 + jnp.exp(-gate)) * uacc[:, cols]).astype(BF16)

    def send_from_ends(q, j):
        @pl.when(me == 0)
        def _():
            rout[q, j] = part[j, rows_of(q), :].astype(BF16)
            r_copy(q, j).start()

        @pl.when(me == n - 1)
        def _():
            lout[q, j] = part[j, rows_of(q), :].astype(BF16)
            l_copy(q, j).start()

    @loop(0, chunks)
    def _(j):
        weight(2, j).wait()
        part[j] = jnp.dot(hid[...], wd[j], preferred_element_type=F32)
        for q in range(pairs):
            @pl.when(q != pair)
            def _():
                send_from_ends(q, j)

    @loop(0, chunks)
    def _(j):
        send_from_ends(pair, j)

    @loop(0, chunks)
    def _(j):
        for q in range(pairs):
            @pl.when(has_left & (me <= 2 * q))
            def _():
                r_copy(q, j).wait_recv()
                value = part[j, rows_of(q), :] + rin[q, j].astype(F32)
                part[j, rows_of(q), :] = value
                rout[q, j] = value.astype(BF16)
                r_copy(q, j).start()

            @pl.when(has_right & (me >= 2 * q + 1))
            def _():
                l_copy(q, j).wait_recv()
                value = part[j, rows_of(q), :] + lin[q, j].astype(F32)
                part[j, rows_of(q), :] = value
                lout[q, j] = value.astype(BF16)
                l_copy(q, j).start()

    @loop(0, chunks)
    def _(j):
        def place(other):
            down = part[j, rows_of(pair), :] + other.astype(F32)
            scaled = (row_share * down).astype(BF16)
            cols = pl.ds(pl.multiple_of(j * width, width), width)
            out_ref[:, cols] = lax.dot_general(
                pick_half, scaled, (((0,), (0,)), ((), ())), preferred_element_type=F32
            ).astype(BF16)

        @pl.when(odd == 0)
        def _():
            l_copy(pair, j).wait_recv()
            place(lin[pair, j])

        @pl.when(odd == 1)
        def _():
            r_copy(pair, j).wait_recv()
            place(rin[pair, j])

    @loop(0, chunks)
    def _(k):
        raw_copy(k).wait_send()

        @pl.when(((odd == 1) & has_right) | ((odd == 0) & has_left))
        def _():
            x_copy(pair, k, partner).wait_send()

        for q in range(pairs):
            @pl.when(forwards(q))
            def _():
                x_copy(q, k, partner).wait_send()

            @pl.when(me <= 2 * q)
            def _():
                r_copy(q, k).wait_send()

            @pl.when(me >= 2 * q + 1)
            def _():
                l_copy(q, k).wait_send()


def shards(n, tokens, w_gate, w_up, w_down, route_ids, route_prob, slot_index):
    count, model = tokens.shape
    hidden = w_gate.shape[1]
    cap = count // 2
    pairs = n // 2
    rows = pairs * cap
    width = 512
    chunks = model // width
    flow = pltpu.VMEM((pairs, chunks, cap, width), BF16)
    dma = pltpu.SemaphoreType.DMA
    vmem = pl.BlockSpec(memory_space=pltpu.VMEM)
    hbm = pl.BlockSpec(memory_space=pl.ANY)
    return pl.pallas_call(
        functools.partial(kernel, n),
        out_shape=jax.ShapeDtypeStruct((count, model), BF16),
        in_specs=[vmem] * 4 + [hbm] * 3,
        out_specs=vmem,
        scratch_shapes=[
            pltpu.VMEM((chunks, width, hidden), BF16),
            pltpu.VMEM((chunks, width, hidden), BF16),
            pltpu.VMEM((chunks, hidden, width), BF16),
            pltpu.VMEM((chunks, cap, width), BF16),
            pltpu.VMEM((chunks, cap, width), BF16),
            pltpu.VMEM((chunks, rows, width), BF16),
            pltpu.VMEM((rows, hidden), F32),
            pltpu.VMEM((rows, hidden), F32),
            pltpu.VMEM((rows, hidden), BF16),
            pltpu.VMEM((chunks, rows, width), F32),
            flow, flow, flow, flow,
            dma((3, chunks)),
            dma((chunks,)), dma((chunks,)),
            dma((pairs, chunks)), dma((pairs, chunks)),
            dma((pairs, chunks)), dma((pairs, chunks)),
            dma((pairs, chunks)), dma((pairs, chunks)),
        ],
        compiler_params=pltpu.CompilerParams(
            collective_id=0, has_side_effects=True, vmem_limit_bytes=60 * 2**20
        ),
        cost_estimate=pl.CostEstimate(
            flops=6 * pairs * cap * model * hidden,
            bytes_accessed=6 * model * hidden,
            transcendentals=pairs * cap * hidden,
        ),
    )(slot_index[None, :], route_ids.T, route_prob[None, :], tokens, w_gate, w_up, w_down)


def solution(mesh):
    return jax.shard_map(
        functools.partial(shards, mesh.shape["expert"]),
        mesh=mesh,
        in_specs=(
            P(("dp", "expert"), None),
            P(None, "expert"),
            P(None, "expert"),
            P("expert", None),
            P(("dp", "expert"), None),
            P(("dp", "expert")),
            P(("dp", "expert")),
        ),
        out_specs=P(("dp", "expert"), None),
        check_vma=False,
    )
```
